32 devices in a mesh: dp: 16 (over z, x, core), tensor: 2 (over y).
Axes of the slice: x: 2, y: 2, z: 4, core: 2. Of those that a mesh axis runs over, the one named last changes fastest.
Arguments:
- inputs: bfloat16 [32768, 1024], P(('dp', 'tensor')), may hold values from -6 to 6
- attn_gain: bfloat16 [1024], P('dp'), may hold values from 0.5 to 1.5
- w_mix_in: bfloat16 [1024, 8, 768], P('dp', 'tensor'), may hold values from -0.1875 to 0.1875
- w_decay_beta: bfloat16 [1024, 8, 2], P('dp', 'tensor'), may hold values from -0.1875 to 0.1875
- conv_weight: float32 [4, 8, 512], P(None, 'tensor'), may hold values from -3 to 3
- a_log: float32 [8], P('tensor'), may hold values from -6 to 2.8
- dt_bias: float32 [8], P('tensor'), may hold values from -6.9 to -2.3
- head_gain: bfloat16 [256], P('dp'), may hold values from 0.5 to 1.5
- w_out: bfloat16 [8, 256, 1024], P('tensor', None, 'dp'), may hold values from -0.25 to 0.25
- mlp_gain: bfloat16 [1024], P('dp'), may hold values from 0.5 to 1.5
- w_gate_up: bfloat16 [1024, 2, 2816], P('dp', None, 'tensor'), may hold values from -0.1875 to 0.1875
- w_down: bfloat16 [2816, 1024], P('tensor', 'dp'), may hold values from -0.21875 to 0.21875
- cotangent: bfloat16 [32768, 1024], P(('dp', 'tensor')), may hold values from -6 to 6
Outputs:
- block_output: bfloat16 [32768, 1024], P(('dp', 'tensor'))
- input_grad: bfloat16 [32768, 1024], P(('dp', 'tensor'))
- attn_gain_grad: float32 [1024], P('dp')
- mix_in_grad: float32 [1024, 8, 768], P('dp', 'tensor')
- decay_beta_grad: float32 [1024, 8, 2], P('dp', 'tensor')
- conv_grad: float32 [4, 8, 512], P(None, 'tensor')
- a_log_grad: float32 [8], P('tensor')
- dt_bias_grad: float32 [8], P('tensor')
- head_gain_grad: float32 [256], P('dp')
- out_grad: float32 [8, 256, 1024], P('tensor', None, 'dp')
- mlp_gain_grad: float32 [1024], P('dp')
- gate_up_grad: float32 [1024, 2, 2816], P('dp', None, 'tensor')
- down_grad: float32 [2816, 1024], P('tensor', 'dp')
The draws below stay inside these ranges and needn't reach their ends.
All inputs are finite; a program needn't handle non-finite values.
Results may differ from the reference program's by a relative error of at most 0.02.
Values may be sent and summed in bfloat16 or wider, within the bound.
A program may use at most 512 MiB of HBM per device.

```python
import jax
import jax.numpy as jnp
from jax import lax

D = 1024
H = 8
DK = 128
DV = 256
FF = 2816
CONV = 4
LEN = 2048
BLOCK = 64
GROUP_ROWS = 2048
TOKENS = 32768
N_DP = 16


def strengthened(values, key, source, target, blocks, factor):
    def block_of(axis_at):
        return (jnp.arange(values.shape[axis_at]) // (values.shape[axis_at] // blocks)).reshape((-1,) + (1,) * (values.ndim - 1 - axis_at))

    first = jax.random.permutation(key, blocks)[block_of(target)]
    far = (block_of(target) + blocks // 2) % blocks
    return jnp.where((block_of(source) == first) | (block_of(source) == far), factor * values, values)


def block_levels(rng, extent, cuts, low, largest):
    gain = 1.0
    for position, shards_of in cuts:
        heights = jax.random.uniform(jax.random.fold_in(jax.random.fold_in(rng, 6), position), (shards_of,), jnp.float32, low / len(cuts), largest / len(cuts))
        gain = gain * jnp.repeat(jnp.exp(heights), extent[position] // shards_of).reshape((-1,) + (1,) * (len(extent) - 1 - position))
    return gain


def centred(stream_key, shape, deviation, reach, cuts=(), held_as=jnp.bfloat16):
    values = deviation * jax.random.normal(stream_key, shape, jnp.float32)
    if cuts:
        values = values * block_levels(stream_key, shape, cuts, -0.22, 0.18)
    return jnp.clip(values, -reach, reach).astype(held_as)


def gaussian_with(key, shape, width, limit, shards, heavy, kind=jnp.bfloat16):
    values = width * jax.random.normal(key, shape, jnp.float32)
    if shards:
        values = values * block_levels(key, shape, shards, -0.22, 0.18)
    return jnp.clip(strengthened(values, jax.random.fold_in(key, 3), *heavy), -limit, limit).astype(kind)


def setup_inputs(seed: int = 0) -> dict:
    arg_keys = jax.random.split(jax.random.key(seed), 14)
    inputs = centred(arg_keys[0], (TOKENS, D), 1.0, 6.0, ((0, 32),))
    attn_gain = jnp.clip(1.0 + 0.1 * jax.random.normal(arg_keys[1], (D,), jnp.float32), 0.5, 1.5).astype(jnp.bfloat16)
    w_mix_in = centred(arg_keys[2], (D, H, 2 * DK + 2 * DV), D ** -0.5, 0.1875, ((0, 16), (1, 2)))
    w_decay_beta = centred(arg_keys[3], (D, H, 2), D ** -0.5, 0.1875, ((0, 16), (1, 2)))
    conv_weight = centred(arg_keys[4], (CONV, H, 2 * DK + DV), 0.5, 3.0, ((1, 2),), jnp.float32)
    a_log = jnp.clip(-6.0 + 8.8 * jax.random.uniform(arg_keys[5], (H,), jnp.float32) ** block_levels(arg_keys[5], (H,), ((0, 2),), -0.2, 0.2), -6.0, 2.8)
    dt_bias = jnp.clip(-6.9 + 4.6000001430511475 * jax.random.uniform(arg_keys[6], (H,), jnp.float32) ** block_levels(arg_keys[6], (H,), ((0, 2),), -0.2, 0.2), -6.9, -2.3)
    head_gain = jnp.clip(1.0 + 0.1 * jax.random.normal(arg_keys[7], (DV,), jnp.float32), 0.5, 1.5).astype(jnp.bfloat16)
    w_out = centred(arg_keys[8], (H, DV, D), (H * DV // 4) ** -0.5, 0.25, ((0, 2), (2, 16)))
    mlp_gain = jnp.clip(1.0 + 0.1 * jax.random.normal(arg_keys[9], (D,), jnp.float32), 0.5, 1.5).astype(jnp.bfloat16)
    w_gate_up = centred(arg_keys[10], (D, 2, FF), D ** -0.5, 0.1875, ((0, 16), (2, 2)))
    w_down = centred(arg_keys[11], (FF, D), (FF // 4) ** -0.5, 0.21875, ((0, 2), (1, 16)))
    cotangent = gaussian_with(arg_keys[12], (TOKENS, D), 1.0, 6.0, ((0, 32),), (0, 1, 32, 2.75))
    return dict(inputs=inputs, attn_gain=attn_gain, w_mix_in=w_mix_in, w_decay_beta=w_decay_beta, conv_weight=conv_weight, a_log=a_log, dt_bias=dt_bias, head_gain=head_gain, w_out=w_out, mlp_gain=mlp_gain, w_gate_up=w_gate_up, w_down=w_down, cotangent=cotangent)


EPSILON = 1e-06
highest = lax.Precision.HIGHEST

@jax.custom_vjp
def low(v):
    return lax.optimization_barrier(v.astype(jnp.bfloat16)).astype(jnp.float32)

@jax.custom_vjp
def low_back(v):
    return v

def low_keep(v):
    return (low(v), None)

def low_pass(kept, grad):
    return (grad,)

def back_keep(v):
    return (v, None)

def back_low(kept, grad):
    return (low(grad),)
low.defvjp(low_keep, low_pass)
low_back.defvjp(back_keep, back_low)

def rms_scale(rows):
    return rows * lax.rsqrt(lax.optimization_barrier(jnp.mean(rows * rows, axis=-1, keepdims=True)) + EPSILON)

def unit_rows(rows):
    return rows * lax.rsqrt(lax.optimization_barrier(jnp.sum(rows * rows, axis=-1, keepdims=True)) + EPSILON)

def matmul(left, right):
    return jnp.dot(left.astype(jnp.float32), right.astype(jnp.float32), preferred_element_type=jnp.float32, precision=highest)

def delta_rule(queries, keys, values, beta, logdecay):
    size = keys.shape[2]
    key_width = keys.shape[3]
    cumulative = jnp.cumsum(logdecay, axis=2)
    order = jnp.arange(size)
    strict = order[:, None] > order[None, :]
    inclusive = order[:, None] >= order[None, :]
    spread = cumulative[:, :, :, None] - cumulative[:, :, None, :]
    below = jnp.where(strict, jnp.exp(jnp.where(strict, spread, 0.0)), 0.0)
    within = jnp.where(inclusive, jnp.exp(jnp.where(inclusive, spread, 0.0)), 0.0)
    decay_now = jnp.exp(cumulative)
    decay_tail = jnp.exp(cumulative[:, :, -1:] - cumulative)
    key_dots = jnp.einsum('bnck,bnjk->bncj', keys, keys, precision=highest)
    system = jnp.eye(size, dtype=jnp.float32) + beta[:, :, :, None] * key_dots * below
    right = jnp.concatenate([(beta * decay_now)[..., None] * keys, beta[..., None] * values], axis=-1)
    solved = jax.scipy.linalg.solve_triangular(system, right, lower=True, unit_diagonal=True)
    weights_w = solved[..., :key_width]
    fresh = solved[..., key_width:]
    tail_keys = decay_tail[..., None] * keys
    block_decay = decay_now[:, :, -1]

    def advance(state, pieces):
        piece_w, piece_fresh, piece_keys, piece_decay = pieces
        updates = piece_fresh - jnp.einsum('bck,bkv->bcv', piece_w, state, precision=highest)
        following = piece_decay[:, None, None] * state + jnp.einsum('bck,bcv->bkv', piece_keys, updates, precision=highest)
        return (following, (state, updates))
    start = jnp.zeros((keys.shape[0], key_width, values.shape[3]), jnp.float32)
    moved = tuple((jnp.moveaxis(array, 1, 0) for array in (weights_w, fresh, tail_keys, block_decay)))
    ending, (states, updates) = lax.scan(advance, start, moved)
    states = jnp.moveaxis(states, 0, 1)
    updates = jnp.moveaxis(updates, 0, 1)
    query_dots = jnp.einsum('bnck,bnjk->bncj', queries, keys, precision=highest) * within
    carried = jnp.einsum('bnck,bnkv->bncv', decay_now[..., None] * queries, states, precision=highest)
    return carried + jnp.einsum('bncj,bnjv->bncv', query_dots, updates, precision=highest)

def mix_core(mixed_in, small, conv_weight, a_log, dt_bias, head_gain):
    count, heads, columns = mixed_in.shape
    conv_width = conv_weight.shape[2]
    seqs = count // LEN
    conv_in = mixed_in[:, :, :conv_width].reshape(seqs, LEN, heads * conv_width)
    kernel = conv_weight.reshape(CONV, heads * conv_width)
    padded = jnp.pad(conv_in, ((0, 0), (CONV - 1, 0), (0, 0)))
    mixed = padded[:, 0:LEN] * kernel[0]
    for offset in range(1, CONV):
        mixed = mixed + padded[:, offset:offset + LEN] * kernel[offset]
    active = jax.nn.silu(mixed).reshape(count, heads, conv_width)
    queries = unit_rows(active[:, :, :DK]) * DK ** (-0.5)
    keys = unit_rows(active[:, :, DK:2 * DK])
    values = active[:, :, 2 * DK:]
    beta = jax.nn.sigmoid(small[:, :, 1])
    logdecay = -jnp.exp(a_log) * jax.nn.softplus(small[:, :, 0] + dt_bias)

    def blocks(array):
        rest = array.shape[2:]
        shaped = array.reshape((seqs, LEN // BLOCK, BLOCK, heads) + rest)
        moved = jnp.moveaxis(shaped, 3, 1)
        return moved.reshape((seqs * heads, LEN // BLOCK, BLOCK) + rest)
    outputs = delta_rule(blocks(queries), blocks(keys), blocks(values), blocks(beta), blocks(logdecay))
    outputs = jnp.moveaxis(outputs.reshape(seqs, heads, LEN, DV), 1, 2).reshape(count, heads, DV)
    gate = mixed_in[:, :, conv_width:]
    return rms_scale(outputs) * head_gain * jax.nn.silu(gate)

def mixer_branch(rows, attn_gain, w_mix_in, w_decay_beta, conv_weight, a_log, dt_bias, head_gain, w_out):
    count = rows.shape[0]
    normed = low(rms_scale(rows) * attn_gain)
    mixed_in = low_back(matmul(normed, w_mix_in.reshape(D, H * (2 * DK + 2 * DV)))).reshape(count, H, 2 * DK + 2 * DV)
    small = low_back(matmul(normed, w_decay_beta.reshape(D, 2 * H))).reshape(count, H, 2)
    gated = low(mix_core(mixed_in, small, conv_weight, a_log, dt_bias, head_gain))
    return low_back(matmul(gated.reshape(count, H * DV), w_out.reshape(H * DV, D)))

def mlp_branch(rows, mlp_gain, w_gate_up, w_down):
    normed = low(rms_scale(rows) * mlp_gain)
    both = low_back(matmul(normed, w_gate_up.reshape(D, 2 * FF)))
    hidden = low(jax.nn.silu(both[:, :FF]) * both[:, FF:])
    return matmul(hidden, w_down)

def block(rows, attn_gain, w_mix_in, w_decay_beta, conv_weight, a_log, dt_bias, head_gain, w_out, mlp_gain, w_gate_up, w_down):
    middle = rows + mixer_branch(rows, attn_gain, w_mix_in, w_decay_beta, conv_weight, a_log, dt_bias, head_gain, w_out)
    return middle + mlp_branch(middle, mlp_gain, w_gate_up, w_down)

def reference(inputs, attn_gain, w_mix_in, w_decay_beta, conv_weight, a_log, dt_bias, head_gain, w_out, mlp_gain, w_gate_up, w_down, cotangent):
    weights = tuple((array.astype(jnp.float32) for array in (attn_gain, w_mix_in, w_decay_beta, conv_weight, a_log, dt_bias, head_gain, w_out, mlp_gain, w_gate_up, w_down)))

    def one_group(totals, group):
        rows, back = group
        result, pullback = jax.vjp(block, rows, *weights)
        grads = pullback(back)
        summed = tuple((total + grad for total, grad in zip(totals, grads[1:])))
        return (summed, (result.astype(jnp.bfloat16), grads[0].astype(jnp.bfloat16)))
    groups = (inputs.astype(jnp.float32).reshape(N_DP, GROUP_ROWS, D), cotangent.astype(jnp.float32).reshape(N_DP, GROUP_ROWS, D))
    start = tuple((jnp.zeros_like(array) for array in weights))
    totals, (results, input_grads) = lax.scan(one_group, start, groups)
    return (results.reshape(TOKENS, D), input_grads.reshape(TOKENS, D), totals[0], totals[1], totals[2], totals[3], totals[4], totals[5], totals[6], totals[7], totals[8], totals[9], totals[10])
```

```python
import functools

import jax
import jax.numpy as jnp
from jax import lax
from jax.experimental import pallas as pl
from jax.experimental.pallas import tpu as pltpu
from jax.sharding import PartitionSpec as P

DK = 128
DV = 256
CONV = 4
LEN = 2048
T_PASSES = 3
K_PASSES = 3
PASSES = 1
CHUNK = 128
STEPS = 8
LANES = 128
EPSILON = 1e-06
highest = lax.Precision.HIGHEST


def rms_scale(rows):
    return rows * lax.rsqrt(jnp.mean(rows * rows, axis=-1, keepdims=True) + EPSILON)


def rms_back(rows, gain, grad):
    scale = lax.rsqrt(jnp.mean(rows * rows, axis=-1, keepdims=True) + EPSILON)
    normed = rows * scale
    weighted = grad * gain
    back = scale * (weighted - normed * jnp.mean(weighted * normed, axis=-1, keepdims=True))
    return (back, jnp.sum(grad * normed, axis=0))


def matmul(left, right):
    return jnp.dot(left, right, preferred_element_type=jnp.float32)


def contract_rows(left, right):
    return lax.dot_general(
        left, right, (((0,), (0,)), ((), ())), preferred_element_type=jnp.float32
    )


def contract_last(left, right):
    return lax.dot_general(
        left, right, (((1,), (1,)), ((), ())), preferred_element_type=jnp.float32
    )


def dot(left, right, dims, passes):
    numbers = (((dims[0],), (dims[1],)), ((), ()))

    def one(first, second):
        return lax.dot_general(first, second, numbers, preferred_element_type=jnp.float32)

    if passes == 6:
        return lax.dot_general(
            left, right, numbers, precision=highest, preferred_element_type=jnp.float32
        )
    left_high = left.astype(jnp.bfloat16)
    right_high = right.astype(jnp.bfloat16)
    total = one(left_high, right_high)
    if passes == 3:
        left_low = (left - left_high.astype(jnp.float32)).astype(jnp.bfloat16)
        right_low = (right - right_high.astype(jnp.float32)).astype(jnp.bfloat16)
        total = total + one(left_high, right_low) + one(left_low, right_high)
    return total


def indices(size):
    shape = (size, size)
    return (
        lax.broadcasted_iota(jnp.int32, shape, 0),
        lax.broadcasted_iota(jnp.int32, shape, 1),
    )


def sigmoid(value):
    return 1.0 / (1.0 + jnp.exp(-value))


def softplus(value):
    return jnp.maximum(value, 0.0) + jnp.log1p(jnp.exp(-jnp.abs(value)))


def inverses(lowers):
    size = lowers[0].shape[0]
    row, col = indices(size)
    eye = jnp.where(row == col, 1.0, 0.0)
    level = 1
    founds = [eye - jnp.where((row >> 1) == (col >> 1), lower, 0.0) for lower in lowers]
    while (1 << level) < size:
        mask = ((row >> (level + 1)) == (col >> (level + 1))) & ((row >> level) != (col >> level))
        parts = [
            dot(found, jnp.where(mask, lower, 0.0), (1, 0), T_PASSES)
            for found, lower in zip(founds, lowers)
        ]
        founds = [
            found - dot(part, found, (1, 0), T_PASSES) for found, part in zip(founds, parts)
        ]
        level += 1
    return founds


def decays(small, par):
    row, col = indices(CHUNK)
    pre = small + par[1:2]
    logdecay = par[0:1] * softplus(pre)
    cumulative = dot(jnp.where(row >= col, 1.0, 0.0), logdecay, (1, 0), 6)
    return pre, logdecay, cumulative, jnp.transpose(cumulative)


def convolve(window, conv, columns):
    total = window[5 : 5 + CHUNK, columns] * conv[0:1, columns]
    for tap in range(1, CONV):
        total = total + window[5 + tap : 5 + tap + CHUNK, columns] * conv[tap : tap + 1, columns]
    return total


def unit(rows):
    scale = lax.rsqrt(jnp.sum(rows * rows, axis=-1, keepdims=True) + EPSILON)
    return rows * scale, scale


def unit_back(normed, scale, grad):
    return scale * (grad - normed * jnp.sum(grad * normed, axis=-1, keepdims=True))


def spread_of(cumulative, flipped, head):
    row, col = indices(CHUNK)
    column = cumulative[:, 2 * head : 2 * head + 1]
    across = flipped[2 * head : 2 * head + 1, :]
    inside = row >= col
    within = jnp.where(inside, jnp.exp(jnp.where(inside, column - across, 0.0)), 0.0)
    last = column[CHUNK - 1 : CHUNK]
    return within, jnp.exp(column), jnp.exp(last - column), jnp.exp(last)


def forward_kernel(
    heads, mixed, conv, par, head_gain, gated, states, solves, state, window
):
    width = 2 * DK + DV
    per_head = width + DV
    row, col = indices(CHUNK)

    @pl.when(pl.program_id(1) == 0)
    def _():
        state[...] = jnp.zeros_like(state)
        window[CHUNK : CHUNK + STEPS] = jnp.zeros((STEPS, heads * width), jnp.float32)

    window[0:STEPS] = window[CHUNK : CHUNK + STEPS]
    states[0] = state[...]
    small_rows = mixed[:, heads * per_head :]
    pre, logdecay, cumulative, flipped = decays(small_rows, par[...])
    betas = sigmoid(small_rows)
    kept = []
    for head in range(heads):
        columns = slice(head * width, (head + 1) * width)
        window[STEPS : STEPS + CHUNK, columns] = mixed[:, head * per_head : head * per_head + width]
        mixed_rows = convolve(window, conv, columns)
        active = mixed_rows * sigmoid(mixed_rows)
        queries = unit(active[:, :DK])[0] * DK ** (-0.5)
        keys = unit(active[:, DK : 2 * DK])[0]
        beta = betas[:, 2 * head + 1 : 2 * head + 2]
        within, now, tail, whole = spread_of(cumulative, flipped, head)
        dots = dot(keys, keys, (1, 1), K_PASSES)
        lower = jnp.where(row > col, beta * dots * within, 0.0)
        kept.append((queries, keys, active[:, 2 * DK :], beta, within, now, tail, whole, lower))
    founds = inverses([entry[-1] for entry in kept])
    for head in range(heads):
        queries, keys, values, beta, within, now, tail, whole, lower = kept[head]
        solves[0, head * CHUNK : (head + 1) * CHUNK] = founds[head]
        start = state[head * DK : (head + 1) * DK]
        both = dot(jnp.concatenate([queries, keys], axis=0), start, (1, 0), PASSES)
        right = beta * (values - now * both[CHUNK:])
        updates = dot(founds[head], right, (1, 0), PASSES)
        attend = dot(queries, keys, (1, 1), PASSES) * within
        outputs = now * both[:CHUNK] + dot(attend, updates, (1, 0), PASSES)
        state[head * DK : (head + 1) * DK] = whole * start + dot(
            tail * keys, updates, (0, 0), PASSES
        )
        gate = mixed[:, head * per_head + width : (head + 1) * per_head]
        normed = outputs * lax.rsqrt(
            jnp.mean(outputs * outputs, axis=-1, keepdims=True) + EPSILON
        )
        gated[:, head * DV : (head + 1) * DV] = (
            normed * head_gain[...] * (gate * sigmoid(gate))
        ).astype(gated.dtype)


def backward_kernel(
    heads,
    mixed,
    before,
    conv,
    par,
    head_gain,
    states,
    solves,
    grads,
    d_mixed,
    d_conv,
    d_par,
    d_gain,
    d_state,
    window,
    d_window,
):
    width = 2 * DK + DV
    per_head = width + DV
    row, col = indices(CHUNK)
    lane = lax.broadcasted_iota(jnp.int32, (CHUNK, LANES), 1)
    step = pl.program_id(1)

    @pl.when((pl.program_id(0) == 0) & (step == 0))
    def _():
        d_conv[...] = jnp.zeros_like(d_conv)
        d_par[...] = jnp.zeros_like(d_par)
        d_gain[...] = jnp.zeros_like(d_gain)

    @pl.when(step == 0)
    def _():
        d_state[...] = jnp.zeros_like(d_state)
        d_window[0:STEPS] = jnp.zeros((STEPS, heads * width), jnp.float32)

    d_window[CHUNK : CHUNK + STEPS] = d_window[0:STEPS]
    first = step == pl.num_programs(1) - 1
    small_rows = mixed[:, heads * per_head :]
    pre, logdecay, cumulative, flipped = decays(small_rows, par[...])
    betas = sigmoid(small_rows)
    d_cumulative = jnp.zeros_like(small_rows)
    d_betas = jnp.zeros_like(small_rows)
    d_last = jnp.zeros((1, LANES), jnp.float32)
    for head in range(heads):
        columns = slice(head * width, (head + 1) * width)
        lead = slice(head * per_head, head * per_head + width)
        window[0:STEPS, columns] = jnp.where(first, 0.0, before[:, lead])
        window[STEPS : STEPS + CHUNK, columns] = mixed[:, lead]
        mixed_rows = convolve(window, conv, columns)
        sigma = sigmoid(mixed_rows)
        active = mixed_rows * sigma
        query_units, query_scale = unit(active[:, :DK])
        queries = query_units * DK ** (-0.5)
        keys, key_scale = unit(active[:, DK : 2 * DK])
        values = active[:, 2 * DK :]
        beta = betas[:, 2 * head + 1 : 2 * head + 2]
        within, now, tail, whole = spread_of(cumulative, flipped, head)
        dots = dot(keys, keys, (1, 1), K_PASSES)
        found = solves[0, head * CHUNK : (head + 1) * CHUNK]
        start = states[0, head * DK : (head + 1) * DK]
        pair = jnp.concatenate([queries, keys], axis=0)
        both = dot(pair, start, (1, 0), PASSES)
        query_start = both[:CHUNK]
        key_start = now * both[CHUNK:]
        free = values - key_start
        updates = dot(found, beta * free, (1, 0), PASSES)
        query_dots = dot(queries, keys, (1, 1), PASSES)
        attend = query_dots * within
        outputs = now * query_start + dot(attend, updates, (1, 0), PASSES)

        gate = mixed[:, head * per_head + width : (head + 1) * per_head]
        gate_sigma = sigmoid(gate)
        silu = gate * gate_sigma
        scale = lax.rsqrt(jnp.mean(outputs * outputs, axis=-1, keepdims=True) + EPSILON)
        normed = outputs * scale
        grad = grads[:, head * DV : (head + 1) * DV]
        gain = head_gain[...]
        along = grad * normed
        d_mixed[:, head * per_head + width : (head + 1) * per_head] = (
            along * gain * (gate_sigma * (1.0 + gate * (1.0 - gate_sigma)))
        ).astype(d_mixed.dtype)
        d_gain[0:1] += jnp.sum(along * silu, axis=0, keepdims=True)
        weighted = grad * gain * silu
        d_out = scale * (
            weighted - normed * jnp.mean(weighted * normed, axis=-1, keepdims=True)
        )

        d_next = d_state[head * DK : (head + 1) * DK]
        tail_keys = tail * keys
        d_updates = dot(attend, d_out, (0, 0), PASSES) + dot(tail_keys, d_next, (1, 0), PASSES)
        d_right = dot(found, d_updates, (0, 0), PASSES)
        d_values = beta * d_right
        d_pair = jnp.concatenate([now * d_out, -now * d_values], axis=0)
        d_state[head * DK : (head + 1) * DK] = whole * d_next + dot(
            pair, d_pair, (0, 0), PASSES
        )
        d_attend = dot(d_out, updates, (1, 1), PASSES) * within
        d_lower = -jnp.where(row > col, dot(d_right, updates, (1, 1), PASSES), 0.0) * within
        d_dots = beta * d_lower
        d_units = dot(d_pair, start, (1, 1), PASSES)
        d_tail_keys = dot(updates, d_next, (1, 1), PASSES)
        d_queries = d_units[:CHUNK] + dot(d_attend, keys, (1, 0), PASSES)
        d_keys = (
            d_units[CHUNK:]
            + dot(d_attend, queries, (0, 0), PASSES)
            + dot(d_dots + jnp.transpose(d_dots), keys, (1, 0), PASSES)
            + tail * d_tail_keys
        )
        d_beta = jnp.sum(d_right * free, axis=-1, keepdims=True) + jnp.sum(
            d_lower * dots, axis=-1, keepdims=True
        )
        moved = d_dots * dots + d_attend * query_dots
        tail_part = jnp.sum(d_tail_keys * tail_keys, axis=-1, keepdims=True)
        d_cum = (
            jnp.sum(moved - jnp.transpose(moved), axis=-1, keepdims=True)
            + now * jnp.sum(d_out * query_start, axis=-1, keepdims=True)
            - jnp.sum(d_values * key_start, axis=-1, keepdims=True)
            - tail_part
        )
        ending = jnp.sum(tail_part, axis=0, keepdims=True) + whole * jnp.sum(
            jnp.sum(d_next * start, axis=-1, keepdims=True), axis=0, keepdims=True
        )
        d_cumulative = jnp.where(lane == 2 * head, d_cum, d_cumulative)
        d_last = jnp.where(lane[0:1] == 2 * head, ending, d_last)
        d_betas = jnp.where(lane == 2 * head + 1, d_beta, d_betas)

        d_active = jnp.concatenate(
            [
                unit_back(query_units, query_scale, d_queries * DK ** (-0.5)),
                unit_back(keys, key_scale, d_keys),
                d_values,
            ],
            axis=1,
        )
        d_rows = d_active * (sigma * (1.0 + mixed_rows * (1.0 - sigma)))
        d_window[0:CHUNK, columns] = d_rows
        d_lead = d_window[3 : 3 + CHUNK, columns] * conv[0:1, columns]
        for tap in range(CONV):
            if tap:
                d_lead = d_lead + (
                    d_window[3 - tap : 3 - tap + CHUNK, columns] * conv[tap : tap + 1, columns]
                )
            d_conv[tap : tap + 1, columns] += jnp.sum(
                d_rows * window[5 + tap : 5 + tap + CHUNK, columns], axis=0, keepdims=True
            )
        d_mixed[:, lead] = d_lead.astype(d_mixed.dtype)

    d_logdecay = dot(jnp.where(row <= col, 1.0, 0.0), d_cumulative, (1, 0), 6) + d_last
    d_logit = d_logdecay * par[0:1] * sigmoid(pre)
    d_mixed[:, heads * per_head :] = (d_logit + d_betas * betas * (1.0 - betas)).astype(
        d_mixed.dtype
    )
    d_par[0:1] += jnp.sum(d_logdecay * logdecay, axis=0, keepdims=True)
    d_par[1:2] += jnp.sum(d_logit, axis=0, keepdims=True)


def core_specs(heads, chunks, backward):
    def at(seq, step):
        place = chunks - 1 - step if backward else step
        return seq * chunks + place

    def rows(columns):
        return pl.BlockSpec((CHUNK, columns), lambda seq, step: (at(seq, step), 0))

    def slab(height, columns):
        return pl.BlockSpec((1, height, columns), lambda seq, step: (at(seq, step), 0, 0))

    def fixed(height, columns):
        return pl.BlockSpec((height, columns), lambda seq, step: (0, 0))

    return at, rows, slab, fixed


def core_forward(mixed, conv, par, head_gain, heads):
    count = mixed.shape[0]
    seqs, chunks = count // LEN, LEN // CHUNK
    width = 2 * DK + DV
    at, rows, slab, fixed = core_specs(heads, chunks, False)
    return pl.pallas_call(
        functools.partial(forward_kernel, heads),
        grid=(seqs, chunks),
        in_specs=[
            rows(mixed.shape[1]),
            fixed(*conv.shape),
            fixed(*par.shape),
            fixed(*head_gain.shape),
        ],
        out_specs=[rows(heads * DV), slab(heads * DK, DV), slab(heads * CHUNK, CHUNK)],
        out_shape=[
            jax.ShapeDtypeStruct((count, heads * DV), jnp.bfloat16),
            jax.ShapeDtypeStruct((seqs * chunks, heads * DK, DV), jnp.float32),
            jax.ShapeDtypeStruct((seqs * chunks, heads * CHUNK, CHUNK), jnp.float32),
        ],
        scratch_shapes=[
            pltpu.VMEM((heads * DK, DV), jnp.float32),
            pltpu.VMEM((CHUNK + STEPS, heads * width), jnp.float32),
        ],
        compiler_params=pltpu.CompilerParams(vmem_limit_bytes=40 * 2**20),
        cost_estimate=pl.CostEstimate(
            flops=count * heads * 600000, bytes_accessed=count * heads * 10000, transcendentals=0
        ),
        name="core_forward",
    )(mixed, conv, par, head_gain)


def core_backward(mixed, conv, par, head_gain, states, solves, grads, heads):
    count = mixed.shape[0]
    seqs, chunks = count // LEN, LEN // CHUNK
    width = 2 * DK + DV
    at, rows, slab, fixed = core_specs(heads, chunks, True)

    def earlier(seq, step):
        return (jnp.maximum(at(seq, step) * (CHUNK // STEPS) - 1, 0), 0)

    return pl.pallas_call(
        functools.partial(backward_kernel, heads),
        grid=(seqs, chunks),
        in_specs=[
            rows(mixed.shape[1]),
            pl.BlockSpec((STEPS, mixed.shape[1]), earlier),
            fixed(*conv.shape),
            fixed(*par.shape),
            fixed(*head_gain.shape),
            slab(heads * DK, DV),
            slab(heads * CHUNK, CHUNK),
            rows(heads * DV),
        ],
        out_specs=[
            rows(mixed.shape[1]),
            fixed(STEPS, conv.shape[1]),
            fixed(*par.shape),
            fixed(STEPS, DV),
        ],
        out_shape=[
            jax.ShapeDtypeStruct(mixed.shape, jnp.bfloat16),
            jax.ShapeDtypeStruct((STEPS, conv.shape[1]), jnp.float32),
            jax.ShapeDtypeStruct(par.shape, jnp.float32),
            jax.ShapeDtypeStruct((STEPS, DV), jnp.float32),
        ],
        scratch_shapes=[
            pltpu.VMEM((heads * DK, DV), jnp.float32),
            pltpu.VMEM((CHUNK + STEPS, heads * width), jnp.float32),
            pltpu.VMEM((CHUNK + STEPS, heads * width), jnp.float32),
        ],
        compiler_params=pltpu.CompilerParams(vmem_limit_bytes=48 * 2**20),
        cost_estimate=pl.CostEstimate(
            flops=count * heads * 900000, bytes_accessed=count * heads * 12000, transcendentals=0
        ),
        name="core_backward",
    )(mixed, mixed, conv, par, head_gain, states, solves, grads)


def spread_lanes(pairs, lanes):
    heads = pairs.shape[0]
    placed = jnp.stack([pairs, jnp.zeros_like(pairs)], axis=1).reshape(1, 2 * heads)
    return jnp.pad(placed, ((0, 0), (0, lanes - 2 * heads)))


def gather_rows(piece):
    return lax.all_gather(piece, "tensor", axis=0, tiled=True)


def row_sums(rows, product):
    size = lax.axis_size("tensor")
    place = lax.axis_index("tensor")
    piece = rows.shape[0] // size

    def part(owner):
        return product(lax.dynamic_slice_in_dim(rows, owner * piece, piece, axis=0))

    arrived = []
    for shift in range(1, size):
        sent = part((place + shift) % size).astype(jnp.bfloat16)
        pairs = [(source, (source + shift) % size) for source in range(size)]
        arrived.append(lax.ppermute(sent, "tensor", pairs))
    total = part(place)
    for received in arrived:
        total = total + received.astype(jnp.float32)
    return total


def scatter_sum(partial_value, axis):
    return lax.psum_scatter(
        partial_value.astype(jnp.bfloat16), "dp", scatter_dimension=axis, tiled=True
    ).astype(jnp.float32)


def per_device(
    inputs,
    attn_gain,
    w_mix_in,
    w_decay_beta,
    conv_weight,
    a_log,
    dt_bias,
    head_gain,
    w_out,
    mlp_gain,
    w_gate_up,
    w_down,
    cotangent,
):
    slices, heads = w_mix_in.shape[:2]
    units = w_gate_up.shape[2]
    width = inputs.shape[1]
    columns = heads * (2 * DK + 2 * DV)
    value_width = head_gain.shape[0]
    padded_gain = jnp.pad(head_gain, (0, slices - value_width))
    packed = jnp.concatenate(
        [
            w_mix_in.reshape(slices, columns),
            w_decay_beta.reshape(slices, 2 * heads),
            jnp.stack([attn_gain, mlp_gain, padded_gain], axis=1),
            jnp.zeros((slices, LANES - 2 * heads - 3), jnp.bfloat16),
        ],
        axis=1,
    )
    all_inputs = gather_rows(inputs)
    mix_matrix = lax.all_gather(packed, "dp", axis=0, tiled=True)
    gains = mix_matrix[:, columns + 2 * heads : columns + 2 * heads + 3].astype(jnp.float32)
    attn_scale = gains[:, 0]
    mlp_scale = gains[:, 1]
    head_scale = gains[:, 2].reshape(-1, slices)[:, :value_width].reshape(1, -1)
    out_matrix = lax.all_gather(w_out.reshape(heads * DV, -1), "dp", axis=1, tiled=True)
    gate_up_matrix = lax.all_gather(
        w_gate_up.reshape(slices, 2 * units), "dp", axis=0, tiled=True
    )
    down_full = lax.all_gather(w_down, "dp", axis=1, tiled=True)
    back_rows = gather_rows(cotangent)

    residual = inputs.astype(jnp.float32)
    normed_one = (rms_scale(all_inputs.astype(jnp.float32)) * attn_scale).astype(jnp.bfloat16)
    mixed = matmul(normed_one, mix_matrix)
    conv = conv_weight.reshape(CONV, -1)
    par = jnp.concatenate(
        [
            spread_lanes(-jnp.exp(a_log), LANES),
            spread_lanes(dt_bias, LANES),
            jnp.zeros((STEPS - 2, LANES), jnp.float32),
        ],
        axis=0,
    )
    gated, states, solves = core_forward(mixed, conv, par, head_scale, heads)
    middle = residual + row_sums(gated, lambda rows: matmul(rows, out_matrix))
    piece_two = (rms_scale(middle) * mlp_scale).astype(jnp.bfloat16)
    normed_two = gather_rows(piece_two)
    both = matmul(normed_two, gate_up_matrix)
    gate = both[:, :units]
    up = both[:, units:]
    hidden = (jax.nn.silu(gate) * up).astype(jnp.bfloat16)
    d_hidden = contract_last(back_rows, down_full)
    sigmoid_gate = jax.nn.sigmoid(gate)
    d_gate = d_hidden * up * sigmoid_gate * (1.0 + gate * (1.0 - sigmoid_gate))
    d_up = d_hidden * gate * sigmoid_gate
    d_both = jnp.concatenate([d_gate, d_up], axis=1).astype(jnp.bfloat16)
    d_normed_two = row_sums(d_both, lambda rows: contract_last(rows, gate_up_matrix))
    gate_up_sum = scatter_sum(contract_rows(normed_two, d_both), 0)
    down_sum = scatter_sum(contract_rows(hidden, back_rows), 1)
    d_middle, grad_mlp_gain = rms_back(middle, mlp_scale, d_normed_two)
    d_middle = d_middle + cotangent.astype(jnp.float32)
    middle_rows = gather_rows(d_middle.astype(jnp.bfloat16))
    hidden_late, middle_rows = lax.optimization_barrier((hidden, middle_rows))
    block_output = (middle + row_sums(hidden_late, lambda rows: matmul(rows, down_full))).astype(
        jnp.bfloat16
    )
    out_sum = scatter_sum(contract_rows(gated, middle_rows), 1)
    d_gated = contract_last(middle_rows, out_matrix)
    d_mixed, d_conv, d_par, d_head = core_backward(
        mixed, conv, par, head_scale, states, solves, d_gated, heads
    )
    mix_sum = scatter_sum(contract_rows(normed_one, d_mixed), 0)
    d_normed_one = row_sums(d_mixed, lambda rows: contract_last(rows, mix_matrix))
    d_inputs, grad_attn_gain = rms_back(residual, attn_scale, d_normed_one)
    input_grad = (d_inputs + d_middle).astype(jnp.bfloat16)

    own = jnp.concatenate([d_conv[:CONV].reshape(-1), d_par[:2].reshape(-1)])
    size = lax.axis_size("tensor")
    place = lax.axis_index("tensor")
    spread = jnp.where(jnp.arange(size)[:, None] == place, own[None], 0.0).reshape(-1)
    sums = lax.psum(
        jnp.concatenate([grad_attn_gain, grad_mlp_gain, d_head[0], spread]), ("dp", "tensor")
    )
    mine = lax.dynamic_slice_in_dim(sums[2 * width + DV :], place * own.shape[0], own.shape[0])
    conv_size = d_conv.shape[1] * CONV
    decays_sum = mine[conv_size:].reshape(2, LANES)[:, : 2 * heads : 2]
    index = lax.axis_index("dp")

    def share(values, length):
        return lax.dynamic_slice_in_dim(values, index * length, length)

    return (
        block_output,
        input_grad,
        share(sums[:width], slices),
        mix_sum[:, :columns].reshape(slices, heads, -1),
        mix_sum[:, columns : columns + 2 * heads].reshape(slices, heads, 2),
        mine[:conv_size].reshape(conv_weight.shape),
        decays_sum[0],
        decays_sum[1],
        share(sums[2 * width : 2 * width + DV], value_width),
        out_sum.reshape(heads, DV, -1),
        share(sums[width : 2 * width], slices),
        gate_up_sum.reshape(slices, 2, units),
        down_sum,
    )


def solution(mesh):
    in_specs = (
        P(("dp", "tensor"), None),
        P("dp"),
        P("dp", "tensor", None),
        P("dp", "tensor", None),
        P(None, "tensor", None),
        P("tensor"),
        P("tensor"),
        P("dp"),
        P("tensor", None, "dp"),
        P("dp"),
        P("dp", None, "tensor"),
        P("tensor", "dp"),
        P(("dp", "tensor"), None),
    )
    out_specs = (
        P(("dp", "tensor"), None),
        P(("dp", "tensor"), None),
        P("dp"),
        P("dp", "tensor", None),
        P("dp", "tensor", None),
        P(None, "tensor", None),
        P("tensor"),
        P("tensor"),
        P("dp"),
        P("tensor", None, "dp"),
        P("dp"),
        P("dp", None, "tensor"),
        P("tensor", "dp"),
    )
    return jax.shard_map(
        per_device, mesh=mesh, in_specs=in_specs, out_specs=out_specs, check_vma=False
    )
```

```python
import functools

import jax
import jax.numpy as jnp
from jax import lax
from jax.experimental import pallas as pl
from jax.experimental.pallas import tpu as pltpu
from jax.sharding import PartitionSpec as P

DK = 128
DV = 256
CONV = 4
LEN = 2048
T_PASSES = 3
K_PASSES = 3
PASSES = 1
CHUNK = 128
STEPS = 8
LANES = 128
EPSILON = 1e-06
highest = lax.Precision.HIGHEST


def rms_scale(rows):
    return rows * lax.rsqrt(jnp.mean(rows * rows, axis=-1, keepdims=True) + EPSILON)


def rms_back(rows, gain, grad):
    scale = lax.rsqrt(jnp.mean(rows * rows, axis=-1, keepdims=True) + EPSILON)
    normed = rows * scale
    weighted = grad * gain
    back = scale * (weighted - normed * jnp.mean(weighted * normed, axis=-1, keepdims=True))
    return (back, jnp.sum(grad * normed, axis=0))


def matmul(left, right):
    return jnp.dot(left, right, preferred_element_type=jnp.float32)


def contract_rows(left, right):
    return lax.dot_general(
        left, right, (((0,), (0,)), ((), ())), preferred_element_type=jnp.float32
    )


def contract_last(left, right):
    return lax.dot_general(
        left, right, (((1,), (1,)), ((), ())), preferred_element_type=jnp.float32
    )


def dot(left, right, dims, passes):
    numbers = (((dims[0],), (dims[1],)), ((), ()))

    def one(first, second):
        return lax.dot_general(first, second, numbers, preferred_element_type=jnp.float32)

    if passes == 6:
        return lax.dot_general(
            left, right, numbers, precision=highest, preferred_element_type=jnp.float32
        )
    left_high = left.astype(jnp.bfloat16)
    right_high = right.astype(jnp.bfloat16)
    total = one(left_high, right_high)
    if passes == 3:
        left_low = (left - left_high.astype(jnp.float32)).astype(jnp.bfloat16)
        right_low = (right - right_high.astype(jnp.float32)).astype(jnp.bfloat16)
        total = total + one(left_high, right_low) + one(left_low, right_high)
    return total


def indices(size):
    shape = (size, size)
    return (
        lax.broadcasted_iota(jnp.int32, shape, 0),
        lax.broadcasted_iota(jnp.int32, shape, 1),
    )


def sigmoid(value):
    return 1.0 / (1.0 + jnp.exp(-value))


def softplus(value):
    return jnp.maximum(value, 0.0) + jnp.log1p(jnp.exp(-jnp.abs(value)))


def inverses(lowers):
    size = lowers[0].shape[0]
    row, col = indices(size)
    eye = jnp.where(row == col, 1.0, 0.0)
    level = 1
    founds = [eye - jnp.where((row >> 1) == (col >> 1), lower, 0.0) for lower in lowers]
    while (1 << level) < size:
        mask = ((row >> (level + 1)) == (col >> (level + 1))) & ((row >> level) != (col >> level))
        parts = [
            dot(found, jnp.where(mask, lower, 0.0), (1, 0), T_PASSES)
            for found, lower in zip(founds, lowers)
        ]
        founds = [
            found - dot(part, found, (1, 0), T_PASSES) for found, part in zip(founds, parts)
        ]
        level += 1
    return founds


def decays(small, par):
    row, col = indices(CHUNK)
    pre = small + par[1:2]
    logdecay = par[0:1] * softplus(pre)
    cumulative = dot(jnp.where(row >= col, 1.0, 0.0), logdecay, (1, 0), 6)
    return pre, logdecay, cumulative, jnp.transpose(cumulative)


def convolve(window, conv, columns):
    total = window[5 : 5 + CHUNK, columns] * conv[0:1, columns]
    for tap in range(1, CONV):
        total = total + window[5 + tap : 5 + tap + CHUNK, columns] * conv[tap : tap + 1, columns]
    return total


def unit(rows):
    scale = lax.rsqrt(jnp.sum(rows * rows, axis=-1, keepdims=True) + EPSILON)
    return rows * scale, scale


def unit_back(normed, scale, grad):
    return scale * (grad - normed * jnp.sum(grad * normed, axis=-1, keepdims=True))


def spread_of(cumulative, flipped, head):
    row, col = indices(CHUNK)
    column = cumulative[:, 2 * head : 2 * head + 1]
    across = flipped[2 * head : 2 * head + 1, :]
    inside = row >= col
    within = jnp.where(inside, jnp.exp(jnp.where(inside, column - across, 0.0)), 0.0)
    last = column[CHUNK - 1 : CHUNK]
    return within, jnp.exp(column), jnp.exp(last - column), jnp.exp(last)


def forward_kernel(
    heads, mixed, conv, par, head_gain, gated, states, solves, state, window
):
    width = 2 * DK + DV
    per_head = width + DV
    row, col = indices(CHUNK)

    @pl.when(pl.program_id(1) == 0)
    def _():
        state[...] = jnp.zeros_like(state)
        window[CHUNK : CHUNK + STEPS] = jnp.zeros((STEPS, heads * width), jnp.float32)

    window[0:STEPS] = window[CHUNK : CHUNK + STEPS]
    states[0] = state[...]
    small_rows = mixed[:, heads * per_head :]
    pre, logdecay, cumulative, flipped = decays(small_rows, par[...])
    betas = sigmoid(small_rows)
    kept = []
    for head in range(heads):
        columns = slice(head * width, (head + 1) * width)
        window[STEPS : STEPS + CHUNK, columns] = mixed[:, head * per_head : head * per_head + width]
        mixed_rows = convolve(window, conv, columns)
        active = mixed_rows * sigmoid(mixed_rows)
        queries = unit(active[:, :DK])[0] * DK ** (-0.5)
        keys = unit(active[:, DK : 2 * DK])[0]
        beta = betas[:, 2 * head + 1 : 2 * head + 2]
        within, now, tail, whole = spread_of(cumulative, flipped, head)
        dots = dot(keys, keys, (1, 1), K_PASSES)
        lower = jnp.where(row > col, beta * dots * within, 0.0)
        kept.append((queries, keys, active[:, 2 * DK :], beta, within, now, tail, whole, lower))
    founds = inverses([entry[-1] for entry in kept])
    for head in range(heads):
        queries, keys, values, beta, within, now, tail, whole, lower = kept[head]
        solves[0, head * CHUNK : (head + 1) * CHUNK] = founds[head]
        start = state[head * DK : (head + 1) * DK]
        both = dot(jnp.concatenate([queries, keys], axis=0), start, (1, 0), PASSES)
        right = beta * (values - now * both[CHUNK:])
        updates = dot(founds[head], right, (1, 0), PASSES)
        attend = dot(queries, keys, (1, 1), PASSES) * within
        outputs = now * both[:CHUNK] + dot(attend, updates, (1, 0), PASSES)
        state[head * DK : (head + 1) * DK] = whole * start + dot(
            tail * keys, updates, (0, 0), PASSES
        )
        gate = mixed[:, head * per_head + width : (head + 1) * per_head]
        normed = outputs * lax.rsqrt(
            jnp.mean(outputs * outputs, axis=-1, keepdims=True) + EPSILON
        )
        gated[:, head * DV : (head + 1) * DV] = (
            normed * head_gain[...] * (gate * sigmoid(gate))
        ).astype(gated.dtype)


def backward_kernel(
    heads,
    mixed,
    before,
    conv,
    par,
    head_gain,
    states,
    solves,
    grads,
    gate_up_part,
    down_part,
    out_part,
    d_mixed,
    d_conv,
    d_par,
    d_gain,
    d_state,
    window,
    d_window,
):
    width = 2 * DK + DV
    per_head = width + DV
    row, col = indices(CHUNK)
    lane = lax.broadcasted_iota(jnp.int32, (CHUNK, LANES), 1)
    step = pl.program_id(1)

    @pl.when((pl.program_id(0) == 0) & (step == 0))
    def _():
        d_conv[...] = jnp.zeros_like(d_conv)
        d_par[...] = jnp.zeros_like(d_par)
        d_gain[...] = jnp.zeros_like(d_gain)

    @pl.when(step == 0)
    def _():
        d_state[...] = jnp.zeros_like(d_state)
        d_window[0:STEPS] = jnp.zeros((STEPS, heads * width), jnp.float32)

    d_window[CHUNK : CHUNK + STEPS] = d_window[0:STEPS]
    first = step == pl.num_programs(1) - 1
    small_rows = mixed[:, heads * per_head :]
    pre, logdecay, cumulative, flipped = decays(small_rows, par[...])
    betas = sigmoid(small_rows)
    d_cumulative = jnp.zeros_like(small_rows)
    d_betas = jnp.zeros_like(small_rows)
    d_last = jnp.zeros((1, LANES), jnp.float32)
    for head in range(heads):
        columns = slice(head * width, (head + 1) * width)
        lead = slice(head * per_head, head * per_head + width)
        window[0:STEPS, columns] = jnp.where(first, 0.0, before[:, lead])
        window[STEPS : STEPS + CHUNK, columns] = mixed[:, lead]
        mixed_rows = convolve(window, conv, columns)
        sigma = sigmoid(mixed_rows)
        active = mixed_rows * sigma
        query_units, query_scale = unit(active[:, :DK])
        queries = query_units * DK ** (-0.5)
        keys, key_scale = unit(active[:, DK : 2 * DK])
        values = active[:, 2 * DK :]
        beta = betas[:, 2 * head + 1 : 2 * head + 2]
        within, now, tail, whole = spread_of(cumulative, flipped, head)
        dots = dot(keys, keys, (1, 1), K_PASSES)
        found = solves[0, head * CHUNK : (head + 1) * CHUNK]
        start = states[0, head * DK : (head + 1) * DK]
        pair = jnp.concatenate([queries, keys], axis=0)
        both = dot(pair, start, (1, 0), PASSES)
        query_start = both[:CHUNK]
        key_start = now * both[CHUNK:]
        free = values - key_start
        updates = dot(found, beta * free, (1, 0), PASSES)
        query_dots = dot(queries, keys, (1, 1), PASSES)
        attend = query_dots * within
        outputs = now * query_start + dot(attend, updates, (1, 0), PASSES)

        gate = mixed[:, head * per_head + width : (head + 1) * per_head]
        gate_sigma = sigmoid(gate)
        silu = gate * gate_sigma
        scale = lax.rsqrt(jnp.mean(outputs * outputs, axis=-1, keepdims=True) + EPSILON)
        normed = outputs * scale
        grad = grads[:, head * DV : (head + 1) * DV]
        gain = head_gain[...]
        along = grad * normed
        d_mixed[:, head * per_head + width : (head + 1) * per_head] = (
            along * gain * (gate_sigma * (1.0 + gate * (1.0 - gate_sigma)))
        ).astype(d_mixed.dtype)
        d_gain[0:1] += jnp.sum(along * silu, axis=0, keepdims=True)
        weighted = grad * gain * silu
        d_out = scale * (
            weighted - normed * jnp.mean(weighted * normed, axis=-1, keepdims=True)
        )

        d_next = d_state[head * DK : (head + 1) * DK]
        tail_keys = tail * keys
        d_updates = dot(attend, d_out, (0, 0), PASSES) + dot(tail_keys, d_next, (1, 0), PASSES)
        d_right = dot(found, d_updates, (0, 0), PASSES)
        d_values = beta * d_right
        d_pair = jnp.concatenate([now * d_out, -now * d_values], axis=0)
        d_state[head * DK : (head + 1) * DK] = whole * d_next + dot(
            pair, d_pair, (0, 0), PASSES
        )
        d_attend = dot(d_out, updates, (1, 1), PASSES) * within
        d_lower = -jnp.where(row > col, dot(d_right, updates, (1, 1), PASSES), 0.0) * within
        d_dots = beta * d_lower
        d_units = dot(d_pair, start, (1, 1), PASSES)
        d_tail_keys = dot(updates, d_next, (1, 1), PASSES)
        d_queries = d_units[:CHUNK] + dot(d_attend, keys, (1, 0), PASSES)
        d_keys = (
            d_units[CHUNK:]
            + dot(d_attend, queries, (0, 0), PASSES)
            + dot(d_dots + jnp.transpose(d_dots), keys, (1, 0), PASSES)
            + tail * d_tail_keys
        )
        d_beta = jnp.sum(d_right * free, axis=-1, keepdims=True) + jnp.sum(
            d_lower * dots, axis=-1, keepdims=True
        )
        moved = d_dots * dots + d_attend * query_dots
        tail_part = jnp.sum(d_tail_keys * tail_keys, axis=-1, keepdims=True)
        d_cum = (
            jnp.sum(moved - jnp.transpose(moved), axis=-1, keepdims=True)
            + now * jnp.sum(d_out * query_start, axis=-1, keepdims=True)
            - jnp.sum(d_values * key_start, axis=-1, keepdims=True)
            - tail_part
        )
        ending = jnp.sum(tail_part, axis=0, keepdims=True) + whole * jnp.sum(
            jnp.sum(d_next * start, axis=-1, keepdims=True), axis=0, keepdims=True
        )
        d_cumulative = jnp.where(lane == 2 * head, d_cum, d_cumulative)
        d_last = jnp.where(lane[0:1] == 2 * head, ending, d_last)
        d_betas = jnp.where(lane == 2 * head + 1, d_beta, d_betas)

        d_active = jnp.concatenate(
            [
                unit_back(query_units, query_scale, d_queries * DK ** (-0.5)),
                unit_back(keys, key_scale, d_keys),
                d_values,
            ],
            axis=1,
        )
        d_rows = d_active * (sigma * (1.0 + mixed_rows * (1.0 - sigma)))
        d_window[0:CHUNK, columns] = d_rows
        d_lead = d_window[3 : 3 + CHUNK, columns] * conv[0:1, columns]
        for tap in range(CONV):
            if tap:
                d_lead = d_lead + (
                    d_window[3 - tap : 3 - tap + CHUNK, columns] * conv[tap : tap + 1, columns]
                )
            d_conv[tap : tap + 1, columns] += jnp.sum(
                d_rows * window[5 + tap : 5 + tap + CHUNK, columns], axis=0, keepdims=True
            )
        d_mixed[:, lead] = d_lead.astype(d_mixed.dtype)

    d_logdecay = dot(jnp.where(row <= col, 1.0, 0.0), d_cumulative, (1, 0), 6) + d_last
    d_logit = d_logdecay * par[0:1] * sigmoid(pre)
    d_mixed[:, heads * per_head :] = (d_logit + d_betas * betas * (1.0 - betas)).astype(
        d_mixed.dtype
    )
    d_par[0:1] += jnp.sum(d_logdecay * logdecay, axis=0, keepdims=True)
    d_par[1:2] += jnp.sum(d_logit, axis=0, keepdims=True)


def core_specs(heads, chunks, backward):
    def at(seq, step):
        place = chunks - 1 - step if backward else step
        return seq * chunks + place

    def rows(columns):
        return pl.BlockSpec((CHUNK, columns), lambda seq, step: (at(seq, step), 0))

    def slab(height, columns):
        return pl.BlockSpec((1, height, columns), lambda seq, step: (at(seq, step), 0, 0))

    def fixed(height, columns):
        return pl.BlockSpec((height, columns), lambda seq, step: (0, 0))

    return at, rows, slab, fixed


def core_forward(mixed, conv, par, head_gain, heads):
    count = mixed.shape[0]
    seqs, chunks = count // LEN, LEN // CHUNK
    width = 2 * DK + DV
    at, rows, slab, fixed = core_specs(heads, chunks, False)
    return pl.pallas_call(
        functools.partial(forward_kernel, heads),
        grid=(seqs, chunks),
        in_specs=[
            rows(mixed.shape[1]),
            fixed(*conv.shape),
            fixed(*par.shape),
            fixed(*head_gain.shape),
        ],
        out_specs=[rows(heads * DV), slab(heads * DK, DV), slab(heads * CHUNK, CHUNK)],
        out_shape=[
            jax.ShapeDtypeStruct((count, heads * DV), jnp.bfloat16),
            jax.ShapeDtypeStruct((seqs * chunks, heads * DK, DV), jnp.float32),
            jax.ShapeDtypeStruct((seqs * chunks, heads * CHUNK, CHUNK), jnp.float32),
        ],
        scratch_shapes=[
            pltpu.VMEM((heads * DK, DV), jnp.float32),
            pltpu.VMEM((CHUNK + STEPS, heads * width), jnp.float32),
        ],
        compiler_params=pltpu.CompilerParams(vmem_limit_bytes=40 * 2**20),
        cost_estimate=pl.CostEstimate(
            flops=count * heads * 600000, bytes_accessed=count * heads * 10000, transcendentals=0
        ),
        name="core_forward",
    )(mixed, conv, par, head_gain)


def core_backward(mixed, conv, par, head_gain, states, solves, grads, heads, earlier_sums):
    count = mixed.shape[0]
    seqs, chunks = count // LEN, LEN // CHUNK
    width = 2 * DK + DV
    at, rows, slab, fixed = core_specs(heads, chunks, True)

    def earlier(seq, step):
        return (jnp.maximum(at(seq, step) * (CHUNK // STEPS) - 1, 0), 0)

    return pl.pallas_call(
        functools.partial(backward_kernel, heads),
        grid=(seqs, chunks),
        in_specs=[
            rows(mixed.shape[1]),
            pl.BlockSpec((STEPS, mixed.shape[1]), earlier),
            fixed(*conv.shape),
            fixed(*par.shape),
            fixed(*head_gain.shape),
            slab(heads * DK, DV),
            slab(heads * CHUNK, CHUNK),
            rows(heads * DV),
        ]
        + [pl.BlockSpec(memory_space=pl.ANY)] * len(earlier_sums),
        out_specs=[
            rows(mixed.shape[1]),
            fixed(STEPS, conv.shape[1]),
            fixed(*par.shape),
            fixed(STEPS, DV),
        ],
        out_shape=[
            jax.ShapeDtypeStruct(mixed.shape, jnp.bfloat16),
            jax.ShapeDtypeStruct((STEPS, conv.shape[1]), jnp.float32),
            jax.ShapeDtypeStruct(par.shape, jnp.float32),
            jax.ShapeDtypeStruct((STEPS, DV), jnp.float32),
        ],
        scratch_shapes=[
            pltpu.VMEM((heads * DK, DV), jnp.float32),
            pltpu.VMEM((CHUNK + STEPS, heads * width), jnp.float32),
            pltpu.VMEM((CHUNK + STEPS, heads * width), jnp.float32),
        ],
        compiler_params=pltpu.CompilerParams(vmem_limit_bytes=48 * 2**20),
        cost_estimate=pl.CostEstimate(
            flops=count * heads * 900000, bytes_accessed=count * heads * 12000, transcendentals=0
        ),
        name="core_backward",
    )(mixed, mixed, conv, par, head_gain, states, solves, grads, *earlier_sums)


def spread_lanes(pairs, lanes):
    heads = pairs.shape[0]
    placed = jnp.stack([pairs, jnp.zeros_like(pairs)], axis=1).reshape(1, 2 * heads)
    return jnp.pad(placed, ((0, 0), (0, lanes - 2 * heads)))


def gather_rows(piece):
    size = lax.axis_size("tensor")
    place = lax.axis_index("tensor")
    rows = piece.shape[0]
    whole = jnp.zeros((size * rows,) + piece.shape[1:], piece.dtype)
    whole = lax.dynamic_update_slice_in_dim(whole, piece, place * rows, axis=0)
    for shift in range(1, size):
        pairs = [(source, (source + shift) % size) for source in range(size)]
        arrived = lax.ppermute(piece, "tensor", pairs)
        owner = (place + size - shift) % size
        whole = lax.dynamic_update_slice_in_dim(whole, arrived, owner * rows, axis=0)
    return whole


def row_sums(rows, product):
    size = lax.axis_size("tensor")
    place = lax.axis_index("tensor")
    piece = rows.shape[0] // size

    def part(owner):
        return product(lax.dynamic_slice_in_dim(rows, owner * piece, piece, axis=0))

    arrived = []
    for shift in range(1, size):
        sent = part((place + shift) % size).astype(jnp.bfloat16)
        pairs = [(source, (source + shift) % size) for source in range(size)]
        arrived.append(lax.ppermute(sent, "tensor", pairs))
    total = part(place)
    for received in arrived:
        total = total + received.astype(jnp.float32)
    return total


def scatter_sum(partial_value, axis):
    return lax.psum_scatter(
        partial_value, "dp", scatter_dimension=axis, tiled=True
    ).astype(jnp.float32)


def row_gradient(left, right):
    return contract_rows(left, right).astype(jnp.bfloat16)


def per_device(
    inputs,
    attn_gain,
    w_mix_in,
    w_decay_beta,
    conv_weight,
    a_log,
    dt_bias,
    head_gain,
    w_out,
    mlp_gain,
    w_gate_up,
    w_down,
    cotangent,
):
    slices, heads = w_mix_in.shape[:2]
    units = w_gate_up.shape[2]
    width = inputs.shape[1]
    columns = heads * (2 * DK + 2 * DV)
    value_width = head_gain.shape[0]
    padded_gain = jnp.pad(head_gain, (0, slices - value_width))
    packed = jnp.concatenate(
        [
            w_mix_in.reshape(slices, columns),
            w_decay_beta.reshape(slices, 2 * heads),
            jnp.stack([attn_gain, mlp_gain, padded_gain], axis=1),
            jnp.zeros((slices, LANES - 2 * heads - 3), jnp.bfloat16),
        ],
        axis=1,
    )
    all_inputs = gather_rows(inputs)
    mix_matrix = lax.all_gather(packed, "dp", axis=0, tiled=True)
    gains = mix_matrix[:, columns + 2 * heads : columns + 2 * heads + 3].astype(jnp.float32)
    attn_scale = gains[:, 0]
    mlp_scale = gains[:, 1]
    head_scale = gains[:, 2].reshape(-1, slices)[:, :value_width].reshape(1, -1)
    out_matrix = lax.all_gather(w_out.reshape(heads * DV, -1), "dp", axis=1, tiled=True)
    gate_up_matrix = lax.all_gather(
        w_gate_up.reshape(slices, 2 * units), "dp", axis=0, tiled=True
    )
    down_full = lax.all_gather(w_down, "dp", axis=1, tiled=True)
    back_rows = gather_rows(cotangent)

    residual = inputs.astype(jnp.float32)
    normed_one = (rms_scale(all_inputs.astype(jnp.float32)) * attn_scale).astype(jnp.bfloat16)
    mixed = matmul(normed_one, mix_matrix)
    conv = conv_weight.reshape(CONV, -1)
    par = jnp.concatenate(
        [
            spread_lanes(-jnp.exp(a_log), LANES),
            spread_lanes(dt_bias, LANES),
            jnp.zeros((STEPS - 2, LANES), jnp.float32),
        ],
        axis=0,
    )
    gated, states, solves = core_forward(mixed, conv, par, head_scale, heads)
    gathered = 0.0 * (back_rows[0, 0] + down_full[0, 0] + gate_up_matrix[0, 0]).astype(jnp.float32)
    middle = (residual + gathered) + row_sums(gated, lambda rows: matmul(rows, out_matrix))
    piece_two = (rms_scale(middle) * mlp_scale).astype(jnp.bfloat16)
    normed_two = gather_rows(piece_two)
    both = matmul(normed_two, gate_up_matrix)
    gate = both[:, :units]
    up = both[:, units:]
    hidden = (jax.nn.silu(gate) * up).astype(jnp.bfloat16)
    d_hidden = contract_last(back_rows, down_full)
    sigmoid_gate = jax.nn.sigmoid(gate)
    d_gate = d_hidden * up * sigmoid_gate * (1.0 + gate * (1.0 - sigmoid_gate))
    d_up = d_hidden * gate * sigmoid_gate
    d_both = jnp.concatenate([d_gate, d_up], axis=1).astype(jnp.bfloat16)
    d_normed_two = row_sums(d_both, lambda rows: contract_last(rows, gate_up_matrix))
    gate_up_part = row_gradient(normed_two, d_both)
    down_part = row_gradient(hidden, back_rows)
    gate_up_sum = scatter_sum(gate_up_part, 0)
    down_sum = scatter_sum(down_part, 1)
    d_middle, grad_mlp_gain = rms_back(middle, mlp_scale, d_normed_two)
    d_middle = d_middle + cotangent.astype(jnp.float32)
    middle_rows = gather_rows(d_middle.astype(jnp.bfloat16))
    hidden_late, middle_rows = lax.optimization_barrier((hidden, middle_rows))
    block_output = (middle + row_sums(hidden_late, lambda rows: matmul(rows, down_full))).astype(
        jnp.bfloat16
    )
    out_part = row_gradient(gated, middle_rows)
    out_sum = scatter_sum(out_part, 1)
    d_gated = contract_last(middle_rows, out_matrix)
    d_mixed, d_conv, d_par, d_head = core_backward(
        mixed, conv, par, head_scale, states, solves, d_gated, heads,
        (gate_up_part, down_part, out_part),
    )
    summed = 0.0 * (gate_up_sum[0, 0] + down_sum[0, 0] + out_sum[0, 0])
    mix_part = (contract_rows(normed_one, d_mixed) + summed).astype(jnp.bfloat16)
    mix_sum = scatter_sum(mix_part, 0)
    d_normed_one = row_sums(d_mixed, lambda rows: contract_last(rows, mix_matrix))
    d_inputs, grad_attn_gain = rms_back(residual, attn_scale, d_normed_one)
    input_grad = (d_inputs + d_middle).astype(jnp.bfloat16)

    own = jnp.concatenate([d_conv[:CONV].reshape(-1), d_par[:2].reshape(-1)])
    own = own + 0.0 * mix_part[0, 0].astype(jnp.float32)
    size = lax.axis_size("tensor")
    place = lax.axis_index("tensor")
    spread = jnp.where(jnp.arange(size)[:, None] == place, own[None], 0.0).reshape(-1)
    sums = lax.psum(
        jnp.concatenate([grad_attn_gain, grad_mlp_gain, d_head[0], spread]), ("dp", "tensor")
    )
    mine = lax.dynamic_slice_in_dim(sums[2 * width + DV :], place * own.shape[0], own.shape[0])
    conv_size = d_conv.shape[1] * CONV
    decays_sum = mine[conv_size:].reshape(2, LANES)[:, : 2 * heads : 2]
    index = lax.axis_index("dp")

    def share(values, length):
        return lax.dynamic_slice_in_dim(values, index * length, length)

    return (
        block_output,
        input_grad,
        share(sums[:width], slices),
        mix_sum[:, :columns].reshape(slices, heads, -1),
        mix_sum[:, columns : columns + 2 * heads].reshape(slices, heads, 2),
        mine[:conv_size].reshape(conv_weight.shape),
        decays_sum[0],
        decays_sum[1],
        share(sums[2 * width : 2 * width + DV], value_width),
        out_sum.reshape(heads, DV, -1),
        share(sums[width : 2 * width], slices),
        gate_up_sum.reshape(slices, 2, units),
        down_sum,
    )


def solution(mesh):
    in_specs = (
        P(("dp", "tensor"), None),
        P("dp"),
        P("dp", "tensor", None),
        P("dp", "tensor", None),
        P(None, "tensor", None),
        P("tensor"),
        P("tensor"),
        P("dp"),
        P("tensor", None, "dp"),
        P("dp"),
        P("dp", None, "tensor"),
        P("tensor", "dp"),
        P(("dp", "tensor"), None),
    )
    out_specs = (
        P(("dp", "tensor"), None),
        P(("dp", "tensor"), None),
        P("dp"),
        P("dp", "tensor", None),
        P("dp", "tensor", None),
        P(None, "tensor", None),
        P("tensor"),
        P("tensor"),
        P("dp"),
        P("tensor", None, "dp"),
        P("dp"),
        P("dp", None, "tensor"),
        P("tensor", "dp"),
    )
    return jax.shard_map(
        per_device, mesh=mesh, in_specs=in_specs, out_specs=out_specs, check_vma=False
    )
```
